256 devices in a mesh: pipe: 8 (over z_lo, y), expert: 32 (over x, z_hi, core).
Axes of the slice: x: 4, y: 4, z: 8 (z_hi: 4, z_lo: 2; z = z_hi * 2 + z_lo), core: 2. Of those that a mesh axis runs over, the one named last changes fastest.
Arguments:
- hold_a: bfloat16 [8, 1024, 3584], P('pipe', 'expert'), may hold values from -48 to 48
- enter_a: bfloat16 [1024, 3584], P('expert'), may hold values from -48 to 48
- saved_b: bfloat16 [2, 8, 1024, 3584], P(None, 'pipe', 'expert'), may hold values from -48 to 48
- hold_g: bfloat16 [8, 1024, 3584], P('pipe', 'expert'), may hold values from -6 to 6
- enter_g: bfloat16 [1024, 3584], P('expert'), may hold values from -6 to 6
- gain: bfloat16 [8, 3584], P('pipe'), may hold values from 0.099609375 to 1.8984375
- w_gate: bfloat16 [8, 3584, 16384], P('pipe', None, 'expert'), may hold values from -0.09375 to 0.09375
- w_up: bfloat16 [8, 3584, 16384], P('pipe', None, 'expert'), may hold values from -0.09375 to 0.09375
- w_down: bfloat16 [8, 16384, 3584], P('pipe', 'expert'), may hold values from -0.1875 to 0.1875
- route_a: int32 [2, 8, 1024, 2], P(None, 'pipe', 'expert'), may hold values from 0 to 15, all different within a row; in each aligned block of 32 rows (0 to 31, 32 to 63, ..., all dimensions but the last counted through in order) at most 6 rows name the same one
- gate_a: int32 [2, 8, 1024, 2], P(None, 'pipe', 'expert'), may hold values from 16 to 255
- route_b: int32 [2, 8, 1024, 2], P(None, 'pipe', 'expert'), may hold values from 0 to 15, all different within a row; in each aligned block of 32 rows (0 to 31, 32 to 63, ..., all dimensions but the last counted through in order) at most 6 rows name the same one
- gate_b: int32 [2, 8, 1024, 2], P(None, 'pipe', 'expert'), may hold values from 16 to 255
Outputs:
- made_out: bfloat16 [2, 8, 1024, 3584], P(None, 'pipe', 'expert')
- grad_out: bfloat16 [2, 8, 1024, 3584], P(None, 'pipe', 'expert')
The draws below stay inside these ranges and needn't reach their ends.
Inputs may be any that keep to these rules, and one draw needn't show every extreme that they name: `route_a`: each row names 2 different experts. Within the 32 rows of one device, for one step and layer, no expert is named more than 6 times, and that count is reached. `route_b`: each row names 2 different experts. Within the 32 rows of one device, for one step and layer, no expert is named more than 6 times, and that count is reached.
All inputs are finite; a program needn't handle non-finite values.
Results may differ from the reference program's by a relative error of at most 0.015.
Values may be sent and summed in bfloat16 or wider, within the bound.
A program may use at most 128 MiB of HBM per device.

```python
import math
import jax
import jax.numpy as jnp
import numpy as np
from jax import lax

D = 3584
HID = 1024
SLICES = 2
HID_DEV = 512
TOP = 2
TOK_DEV = 32
TICKS = 2
EXPERTS = 16
CAP = 6
TOKENS = 1024
LAYERS = 8
N_EXPERT = 32


def spread_rows(key, base_values, lowest, highest):
    row_key, col_key = jax.random.split(key)
    row_scale = jnp.exp(jax.random.uniform(row_key, base_values.shape[:-1] + (1,), jnp.float32, math.log(lowest), math.log(highest)))
    col_scale = jnp.exp(jax.random.uniform(col_key, (base_values.shape[-1],), jnp.float32, math.log(0.5), math.log(2.0)))
    return base_values * row_scale * col_scale[None, :]


def activation_draw(key, array_shape, spread_low, spread_high):
    base_key, scale_key = jax.random.split(key)
    base_values = jnp.clip(jax.random.normal(base_key, array_shape, jnp.float32), -6.0, 6.0)
    return spread_rows(scale_key, base_values, spread_low, spread_high).astype(jnp.bfloat16)


def draw_hold_a(key, part):
    key = jax.random.fold_in(key, 11)
    return activation_draw(key, (LAYERS, TOKENS, D), 0.3, 3.0)


def draw_enter_a(key, part):
    key = jax.random.fold_in(key, 12)
    return activation_draw(key, (TOKENS, D), 0.3, 3.0)


def draw_saved_b(key, part):
    key = jax.random.fold_in(key, 13)
    return activation_draw(key, (TICKS, LAYERS, TOKENS, D), 0.3, 3.0)


def place_ends(drawn, own_key, low, top_value):
    shape = drawn.shape
    place = [jax.random.randint(jax.random.fold_in(own_key, axis), (), 0, shape[axis]) for axis in range(len(shape))]
    drawn = drawn.at[tuple(place)].set(low)
    longest = shape.index(max(shape))
    place[longest] = (place[longest] + 1) % shape[longest]
    return drawn.at[tuple(place)].set(top_value)


def shard_levels(own_key, dims, shards, least, high):
    def one(dim, parts):
        heights = jax.random.uniform(jax.random.fold_in(jax.random.fold_in(own_key, 6), dim), (parts,), jnp.float32, least / len(shards), high / len(shards))
        return jnp.repeat(jnp.exp(heights), dims[dim] // parts).reshape((-1,) + (1,) * (len(dims) - dim - 1))

    factor_of = one(*shards[0])
    for cut in shards[1:]:
        factor_of = factor_of * one(*cut)
    return factor_of


def shared_out(key, own, number, rows, number_of, top, limit, lean):
    ranking = jax.random.permutation(key, number_of)
    heavy_load, common = shares(number_of, rows * top, limit, lean, True), shares(number_of, rows * top, limit, lean, False)
    places = jnp.arange(number_of)

    def named(lengths, turn):
        used = int((lengths > 0).sum())
        fixed = max(1, used // 4)
        shifted = fixed + (places - fixed + turn * (used - fixed)) % max(1, number_of - fixed)
        return jnp.zeros((number_of,), jnp.int32).at[ranking[jnp.where(places < fixed, places, shifted)]].set(jnp.asarray(lengths, jnp.int32))

    lengths = jnp.where(number % 4 == 0, named(heavy_load, number // 4), named(common, number - number // 4 - 1))
    mixed = jax.random.permutation(jax.random.fold_in(own, 3), number_of)
    donor, taker = mixed[0:number_of // 2 * 2:2], mixed[1:number_of // 2 * 2:2]
    room = jnp.minimum(lengths[donor] - 1, limit - lengths[taker]) // 2
    room = jnp.where((donor == ranking[0]) | (taker == ranking[0]) | (lengths[taker] == 0), 0, jnp.maximum(room, 0))
    shifted = jax.random.randint(jax.random.fold_in(own, 4), (number_of // 2,), 0, 1 << 20) % (room + 1)
    lengths = lengths.at[donor].add(-shifted).at[taker].add(shifted)
    labels = jnp.searchsorted(jnp.cumsum(lengths), jnp.arange(rows * top), side="right").astype(jnp.int32)
    table = labels.reshape(top, rows).T
    table = table[jax.random.permutation(jax.random.fold_in(own, 1), rows)]
    turn = jax.random.randint(jax.random.fold_in(own, 2), (rows, 1), 0, top)
    return jnp.take_along_axis(table, (jnp.arange(top)[None, :] + turn) % top, axis=1)


def shares(count, total, bound, slope, full):
    weights = [(1 << 20) // math.isqrt(grade ** slope) + 1 for grade in range(1, count + 1)]
    largest = bound if full else min(bound, max(-(-total // count), total * weights[0] // sum(weights)))
    least = 1 if total - largest >= count - 1 else 0
    counts, rest = [largest] + [least] * (count - 1), total - largest - least * (count - 1)
    while rest > 0:
        movable = [i for i in range(1, count) if counts[i] < largest] or [i for i in range(1, count) if counts[i] < bound]
        whole, left = sum([weights[i] for i in movable]), rest
        for i in movable:
            more = min(bound - counts[i], max(1, left * weights[i] // whole), rest)
            counts[i] = counts[i] + more
            rest = rest - more
    return np.array(counts)


def centred(stream_key, extent, spread, reach, cuts=(), kind=jnp.bfloat16):
    factor_of = shard_levels(stream_key, extent, cuts, -0.22, 0.18) if cuts else 1.0
    values = jax.random.normal(stream_key, extent, jnp.float32) * spread * factor_of
    return jnp.minimum(jnp.maximum(values, -reach), reach).astype(kind)


def setup_inputs(seed: int = 0) -> dict:
    key_list = jax.random.split(jax.random.key(seed), 14)
    hold_a = draw_hold_a(jax.random.fold_in(key_list[13], 71), 0)
    enter_a = draw_enter_a(jax.random.fold_in(key_list[13], 71), 0)
    saved_b = draw_saved_b(jax.random.fold_in(key_list[13], 71), 0)
    hold_g = centred(key_list[3], (LAYERS, TOKENS, D), 1.0, 6.0, ((0, 8), (1, 32)))
    enter_g = centred(key_list[4], (TOKENS, D), 1.0, 6.0, ((0, 32),))
    gain = jnp.clip(1.0 + 0.18 * jax.random.normal(key_list[5], (LAYERS, D), jnp.float32), 0.099609375, 1.8984375).astype(jnp.bfloat16)
    w_gate = centred(key_list[6], (LAYERS, D, EXPERTS * HID), D ** -0.5, 0.09375, ((0, 8), (2, 32)))
    w_up = centred(key_list[7], (LAYERS, D, EXPERTS * HID), D ** -0.5, 0.09375, ((0, 8), (2, 32)))
    w_down = centred(key_list[8], (LAYERS, EXPERTS * HID, D), HID ** -0.5, 0.1875, ((0, 8), (1, 32)))
    route_a_keys = jax.random.split(jax.random.fold_in(key_list[9], 1), TICKS * LAYERS * TOKENS // TOK_DEV)
    route_a_turns = jax.random.permutation(jax.random.fold_in(key_list[9], 3), TICKS * LAYERS * TOKENS // TOK_DEV)
    route_a = jax.vmap(lambda own, number: shared_out(jax.random.fold_in(key_list[9], 2), own, number, TOK_DEV, EXPERTS, TOP, CAP, 1))(route_a_keys, route_a_turns).reshape((TICKS, LAYERS, TOKENS, TOP))
    gate_a = place_ends(jax.random.randint(key_list[10], (TICKS, LAYERS, TOKENS, TOP), 16, 256), jax.random.fold_in(key_list[10], 1), 16, 255).astype(jnp.int32)
    route_b_keys = jax.random.split(jax.random.fold_in(key_list[11], 1), TICKS * LAYERS * TOKENS // TOK_DEV)
    route_b_turns = jax.random.permutation(jax.random.fold_in(key_list[11], 3), TICKS * LAYERS * TOKENS // TOK_DEV)
    route_b = jax.vmap(lambda own, number: shared_out(jax.random.fold_in(key_list[11], 2), own, number, TOK_DEV, EXPERTS, TOP, CAP, 1))(route_b_keys, route_b_turns).reshape((TICKS, LAYERS, TOKENS, TOP))
    gate_b = place_ends(jax.random.randint(key_list[12], (TICKS, LAYERS, TOKENS, TOP), 16, 256), jax.random.fold_in(key_list[12], 1), 16, 255).astype(jnp.int32)
    return dict(hold_a=hold_a, enter_a=enter_a, saved_b=saved_b, hold_g=hold_g, enter_g=enter_g, gain=gain, w_gate=w_gate, w_up=w_up, w_down=w_down, route_a=route_a, gate_a=gate_a, route_b=route_b, gate_b=gate_b)


epsilon = 1e-06
gate_unit = 1.0 / 256.0

def norm_rows(x_rows, gain_row):
    as_float = x_rows.astype(jnp.float32)
    inverse = lax.rsqrt(lax.optimization_barrier(jnp.mean(as_float * as_float, axis=1, keepdims=True)) + epsilon)
    normed = (as_float * inverse * gain_row.astype(jnp.float32)[None, :]).astype(jnp.bfloat16)
    return (as_float, inverse, normed)

def grouped(flat_route, expert_id):
    keys = jnp.where(flat_route == expert_id, 0, 1).astype(jnp.int32)
    ordering = jnp.argsort(keys, stable=True)[:N_EXPERT * CAP].astype(jnp.int32)
    valid_rows = (flat_route[ordering] == expert_id).astype(jnp.float32)
    return (ordering, valid_rows)

def expert_weights(w_gate, w_up, w_down, expert_id):
    gate_cols = lax.dynamic_index_in_dim(w_gate.reshape(D, SLICES, EXPERTS, HID_DEV), expert_id, 2, False)
    up_cols = lax.dynamic_index_in_dim(w_up.reshape(D, SLICES, EXPERTS, HID_DEV), expert_id, 2, False)
    down_rows = lax.dynamic_index_in_dim(w_down.reshape(SLICES, EXPERTS, HID_DEV, D), expert_id, 1, False)
    return (gate_cols, up_cols, down_rows)

def forward_layer(x_rows, gain_row, w_gate, w_up, w_down, route, gate_num):
    as_float, inverse, normed = norm_rows(x_rows, gain_row)
    flat_route = route.reshape(-1)
    gate_value = gate_num.reshape(-1).astype(jnp.float32) * gate_unit
    token_of = jnp.arange(flat_route.shape[0], dtype=jnp.int32) // TOP

    def one_expert(summed, expert_id):
        ordering, valid_rows = grouped(flat_route, expert_id)
        gate_cols, up_cols, down_rows = expert_weights(w_gate, w_up, w_down, expert_id)
        token_rows = normed[token_of[ordering]]
        gate_pre = jnp.dot(token_rows, gate_cols.reshape(D, HID), preferred_element_type=jnp.float32)
        up_pre = jnp.dot(token_rows, up_cols.reshape(D, HID), preferred_element_type=jnp.float32)
        hidden = (gate_pre * jax.nn.sigmoid(gate_pre) * up_pre).astype(jnp.bfloat16)
        pieces = jnp.einsum('rsh,shd->srd', hidden.reshape(-1, SLICES, HID_DEV).astype(jnp.float32), down_rows.astype(jnp.float32)).astype(jnp.bfloat16)
        expert_out = lax.optimization_barrier(jnp.sum(pieces.astype(jnp.float32), axis=0))
        scaled = expert_out * (gate_value[ordering] * valid_rows)[:, None]
        return (summed.at[token_of[ordering]].add(scaled), expert_id)
    summed = lax.scan(one_expert, jnp.zeros((TOKENS, D), jnp.float32), jnp.arange(EXPERTS, dtype=jnp.int32))[0]
    return (as_float + summed).astype(jnp.bfloat16)

def backward_layer(x_rows, cot, gain_row, w_gate, w_up, w_down, route, gate_num):
    as_float, inverse, normed = norm_rows(x_rows, gain_row)
    flat_route = route.reshape(-1)
    gate_value = gate_num.astype(jnp.float32) * gate_unit
    token_of = jnp.arange(flat_route.shape[0], dtype=jnp.int32) // TOP
    cot_float = cot.astype(jnp.float32)
    cot_rows = (gate_value[:, :, None] * cot_float[:, None, :]).astype(jnp.bfloat16).reshape(TOKENS * TOP, D)

    def one_expert(summed, expert_id):
        ordering, valid_rows = grouped(flat_route, expert_id)
        gate_cols, up_cols, down_rows = expert_weights(w_gate, w_up, w_down, expert_id)
        token_rows = normed[token_of[ordering]]
        scaled_rows = cot_rows[ordering]
        gate_pre = jnp.dot(token_rows, gate_cols.reshape(D, HID), preferred_element_type=jnp.float32)
        up_pre = jnp.dot(token_rows, up_cols.reshape(D, HID), preferred_element_type=jnp.float32)
        sigma_gate = jax.nn.sigmoid(gate_pre)
        grad_hidden = jnp.dot(scaled_rows, down_rows.reshape(HID, D).T, preferred_element_type=jnp.float32)
        grad_gate = (grad_hidden * up_pre * sigma_gate * (1.0 + gate_pre * (1.0 - sigma_gate))).astype(jnp.bfloat16)
        grad_up = (grad_hidden * gate_pre * sigma_gate).astype(jnp.bfloat16)
        from_gate = jnp.einsum('rsh,dsh->srd', grad_gate.reshape(-1, SLICES, HID_DEV).astype(jnp.float32), gate_cols.astype(jnp.float32))
        from_up = jnp.einsum('rsh,dsh->srd', grad_up.reshape(-1, SLICES, HID_DEV).astype(jnp.float32), up_cols.astype(jnp.float32))
        pieces = (from_gate + from_up).astype(jnp.bfloat16)
        back_sum = lax.optimization_barrier(jnp.sum(pieces.astype(jnp.float32), axis=0)) * valid_rows[:, None]
        return (summed.at[token_of[ordering]].add(back_sum), expert_id)
    d_normed = lax.scan(one_expert, jnp.zeros((TOKENS, D), jnp.float32), jnp.arange(EXPERTS, dtype=jnp.int32))[0]
    gained = gain_row.astype(jnp.float32)[None, :] * d_normed
    inner = lax.optimization_barrier(jnp.mean(as_float * gained, axis=1, keepdims=True))
    grad_x = cot_float + inverse * gained - as_float * inverse ** 3 * inner
    return grad_x.astype(jnp.bfloat16)

def forward_packed(layer_args):
    return forward_layer(*layer_args)

def backward_packed(layer_args):
    return backward_layer(*layer_args)

def reference(hold_a, enter_a, saved_b, hold_g, enter_g, gain, w_gate, w_up, w_down, route_a, gate_a, route_b, gate_b):
    forward_in = hold_a
    cot_in = hold_g
    made_list = []
    grad_list = []
    for tick_index in range(TICKS):
        layer_out = lax.map(forward_packed, (forward_in, gain, w_gate, w_up, w_down, route_a[tick_index], gate_a[tick_index]))
        grad_in = lax.map(backward_packed, (saved_b[tick_index], cot_in, gain, w_gate, w_up, w_down, route_b[tick_index], gate_b[tick_index]))
        made_list.append(layer_out)
        grad_list.append(grad_in)
        forward_in = jnp.concatenate([enter_a[None], layer_out[:-1]], axis=0)
        cot_in = jnp.concatenate([grad_in[1:], enter_g[None]], axis=0)
    return (jnp.stack(made_list), jnp.stack(grad_list))
```

```python
import functools

import jax
import jax.numpy as jnp
import numpy as np
from jax import lax
from jax.experimental import pallas as pl
from jax.experimental.pallas import tpu as pltpu
from jax.sharding import PartitionSpec as P

SLICES = 2
TOP = 2
TICKS = 2
CAP = 6
MESH = pl.DeviceIdType.MESH
BF = jnp.bfloat16
F32 = jnp.float32

epsilon = 1e-06
gate_unit = 1.0 / 256.0

XN = 4
ZN = 4
PEERS = 8
GROUPS = 4
SLOTS = 48
COL = 128
PART = GROUPS * COL
LAG = 2


def perm_tables():
    r, g, q, s = np.meshgrid(
        np.arange(PEERS), np.arange(GROUPS), np.arange(2), np.arange(CAP), indexing="ij"
    )
    r, g, q, s = (a.reshape(-1) for a in (r, g, q, s))
    zrow = r * SLOTS + g * 2 * CAP + q * CAP + s
    p1 = np.zeros((PEERS * SLOTS, PEERS * SLOTS), np.float32)
    p1[g * 2 * SLOTS + q * SLOTS + r * CAP + s, zrow] = 1.0
    p2 = np.zeros((PEERS * SLOTS, GROUPS * XN * SLOTS), np.float32)
    for dx in range(XN):
        hit = q == dx % 2
        p2[zrow[hit], (g * XN * SLOTS + dx * SLOTS + r * CAP + s)[hit]] = 1.0
    return p1, p2


def place_of(index):
    return index // (ZN * 2), (index // 2) % ZN, index % 2


def route_tables(route, gate):
    number, tokens, top = route.shape
    experts = ZN * 2 * 2
    x, z, c = place_of(lax.axis_index("expert"))
    flat = route.reshape(number, tokens * top)
    matches = (flat[:, :, None] == jnp.arange(experts, dtype=jnp.int32)).astype(jnp.int32)
    before = jnp.cumsum(matches, axis=1) - matches
    slot = flat * CAP + jnp.sum(before * matches, axis=2)
    slot = slot.reshape(number, tokens, top)
    row = np.arange(PEERS * SLOTS)
    r, g, q, s = row // SLOTS, row // (2 * CAP) % GROUPS, row // CAP % 2, row % CAP
    expert = (x + q) % 2 * (ZN * 2) + (z + r // 2) % ZN * 2 + (c + r % 2) % 2
    row_slot = (expert * CAP + s).astype(jnp.int32)
    own_group = (g[:, None] == np.arange(GROUPS * tokens)[None, :] // tokens)
    lanes = jnp.tile(slot.transpose(0, 2, 1), (1, 1, GROUPS))
    gate_lanes = jnp.tile(gate.transpose(0, 2, 1).astype(F32) * gate_unit, (1, 1, GROUPS))
    hit = (lanes[:, :, None, :] == row_slot[None, None, :, None]) & own_group[None, None]
    plain = jnp.sum(hit.astype(F32), axis=1).astype(BF)
    gated = jnp.sum(jnp.where(hit, gate_lanes[:, :, None, :], 0.0), axis=1).astype(BF)
    hit_t = (lanes[:, :, :, None] == row_slot[None, None, None, :]) & own_group.T[None, None]
    plain_t = jnp.sum(hit_t.astype(F32), axis=1).astype(BF)
    gated_t = jnp.sum(jnp.where(hit_t, gate_lanes[:, :, :, None], 0.0), axis=1).astype(BF)
    return plain, gated, plain_t, gated_t


LEG_F0, LEG_B0, LEG_C0, LEG_B1, LEG_F1, LEG_C1 = range(6)
LEGS = 6
RETURNS = 4


def kernel(
    parts,
    hold_a,
    enter_a,
    saved_b,
    hold_g,
    enter_g,
    gain,
    sel,
    comb,
    p1,
    p2,
    wg_hbm,
    wu_hbm,
    wd_hbm,
    made,
    grad,
    wg,
    wu,
    wd,
    xblk,
    sblk,
    cblk,
    nblk,
    inv_b,
    dn,
    perm_f,
    perm_out,
    perm_b,
    zsend,
    zrecv,
    xout,
    xin,
    oute,
    xret,
    zback,
    zret,
    acc,
    acc_c,
    hid,
    w_sem,
    zs_sem,
    zr_sem,
    xs_sem,
    xr_sem,
    ps_sem,
    pr_sem,
):
    n_pipe = lax.axis_size("pipe")
    pipe = lax.axis_index("pipe")
    x, z, c = place_of(lax.axis_index("expert"))
    tokens = hold_a.shape[0]
    width = parts * PART
    blocks = parts * GROUPS

    def along_z(r, sign):
        return (pipe, x * (ZN * 2) + (z + ZN + sign * (r // 2)) % ZN * 2 + (c + r % 2) % 2)

    def along_x(dx, sign):
        return (pipe, (x + XN + sign * dx) % XN * (ZN * 2) + z * 2 + c)

    def along_pipe(sign):
        return ((pipe + n_pipe + sign) % n_pipe, lax.axis_index("expert"))

    weights = [
        pltpu.make_async_copy(wg_hbm, wg, w_sem.at[0]),
        pltpu.make_async_copy(wu_hbm, wu, w_sem.at[1]),
        pltpu.make_async_copy(wd_hbm, wd, w_sem.at[2]),
    ]
    for copy in weights:
        copy.start()

    barrier = pltpu.get_barrier_semaphore()
    greeted = [along_z(r, 1) for r in range(1, PEERS)]
    greeted += [along_x(dx, 1) for dx in range(1, XN)]
    greeted += [along_pipe(1), along_pipe(-1)]
    for peer in greeted:
        pl.semaphore_signal(barrier, inc=1, device_id=peer, device_id_type=MESH)

    def to_blocks(rows, ref, tick):
        for b in range(blocks):
            ref[tick, b] = rows[:, b * COL : (b + 1) * COL]

    def norm_blocks(ref, tick, leg):
        as_float = ref[tick].astype(F32)
        square = jnp.sum(jnp.sum(as_float * as_float, axis=0), axis=1, keepdims=True)
        inverse = lax.rsqrt(square * (1.0 / width) + epsilon)
        for b in range(blocks):
            gain_row = gain[:, b * COL : (b + 1) * COL].astype(F32)
            nblk[leg, b] = (as_float[b] * inverse * gain_row).astype(BF)
        return inverse

    to_blocks(hold_a[...], xblk, 0)
    norm_blocks(xblk, 0, LEG_F0)
    pl.semaphore_wait(barrier, len(greeted))

    def send(src, dst, s_sem, r_sem, peer):
        pltpu.make_async_remote_copy(
            src_ref=src,
            dst_ref=dst,
            send_sem=s_sem,
            recv_sem=r_sem,
            device_id=peer,
            device_id_type=MESH,
        ).start()

    def wait_for(ref, sem):
        pltpu.make_async_copy(ref, ref, sem).wait()

    def between(s, low, high):
        return (s >= low) & (s < high)

    def select(leg, n):
        rows = nblk[leg, pl.ds(n * GROUPS, GROUPS)].reshape(GROUPS * tokens, COL)
        picked = jnp.dot(sel[leg], rows, preferred_element_type=F32).astype(BF)
        picked = picked.reshape(PEERS, SLOTS, COL)
        zrecv[leg, n, 0] = picked[0]
        zsend[leg, n] = picked
        for r in (4, 5, 2, 3, 6, 7, 1):
            send(
                zsend.at[leg, n, r],
                zrecv.at[leg, n, r],
                zs_sem.at[leg],
                zr_sem.at[leg, n],
                along_z(r, 1),
            )

    def spread(leg, n):
        wait_for(zrecv.at[leg, n, pl.ds(1, PEERS - 1)], zr_sem.at[leg, n])
        rows = zrecv[leg, n].reshape(PEERS * SLOTS, COL)
        sorted_rows = jnp.dot(p1[...], rows, preferred_element_type=F32).astype(BF)
        sorted_rows = sorted_rows.reshape(GROUPS, 2, SLOTS, COL)
        for q in (1, 0):
            for g in range(GROUPS):
                xout[leg, n, q, :, g * COL : (g + 1) * COL] = sorted_rows[g, q]
                if q == 0:
                    xin[leg, n, 0, :, g * COL : (g + 1) * COL] = sorted_rows[g, q]
        for dx in (2, 1, 3):
            send(
                xout.at[leg, n, dx % 2],
                xin.at[leg, n, dx],
                xs_sem.at[leg],
                xr_sem.at[leg, n],
                along_x(dx, 1),
            )

    def wait_rows(leg, n):
        wait_for(xin.at[leg, n, pl.ds(1, XN - 1)], xr_sem.at[leg, n])
        return xin[leg, n].reshape(XN * SLOTS, PART)

    def expert_in(leg, n, back):
        rows = wait_rows(leg, n)
        for j, w in enumerate((wg, wu)):
            product = jnp.dot(rows, w[n], preferred_element_type=F32)
            acc[back, j] = jnp.where(n == 0, 0.0, acc[back, j]) + product

    def columns(n):
        return pl.ds(pl.multiple_of(n * PART, PART), PART)

    contract = (((1,), (1,)), ((), ()))

    def expert_cot(leg, n):
        rows = wait_rows(leg, n)
        product = lax.dot_general(rows, wd[:, columns(n)], contract, preferred_element_type=F32)
        acc_c[...] = jnp.where(n == 0, 0.0, acc_c[...]) + product

    def give_back(leg, n, piece):
        piece = piece.astype(BF).reshape(XN, SLOTS, PART)
        xret[leg, n, 0] = piece[0]
        oute[leg, n] = piece
        for dx in (2, 1, 3):
            send(
                oute.at[leg, n, dx],
                xret.at[leg, n, dx],
                xs_sem.at[LEGS + leg],
                xr_sem.at[LEGS + leg, n],
                along_x(dx, -1),
            )

    def out_forward(leg, n):
        give_back(leg, n, jnp.dot(hid[0], wd[:, columns(n)], preferred_element_type=F32))

    def out_backward(leg, n):
        piece = lax.dot_general(hid[1], wg[n], contract, preferred_element_type=F32)
        piece += lax.dot_general(hid[2], wu[n], contract, preferred_element_type=F32)
        give_back(leg, n, piece)

    def gather_back(leg, n):
        wait_for(xret.at[leg, n, pl.ds(1, XN - 1)], xr_sem.at[LEGS + leg, n])
        rows = xret[leg, n].reshape(XN * SLOTS, PART)
        stacked = jnp.concatenate(
            [rows[:, g * COL : (g + 1) * COL] for g in range(GROUPS)], axis=0
        )
        sums = jnp.dot(p2[...], stacked, preferred_element_type=F32).astype(BF)
        sums = sums.reshape(PEERS, SLOTS, COL)
        zret[leg, n, 0] = sums[0]
        zback[leg, n] = sums
        for r in (4, 5, 2, 3, 6, 7, 1):
            send(
                zback.at[leg, n, r],
                zret.at[leg, n, r],
                zs_sem.at[LEGS + leg],
                zr_sem.at[LEGS + leg, n],
                along_z(r, -1),
            )

    def combine(leg, n):
        wait_for(zret.at[leg, n, pl.ds(1, PEERS - 1)], zr_sem.at[LEGS + leg, n])
        rows = zret[leg, n].reshape(PEERS * SLOTS, COL)
        total = jnp.dot(comb[leg], rows, preferred_element_type=F32)
        return total.reshape(GROUPS, tokens, COL)

    def combine_forward(tick, n):
        total = combine(2 * tick, n)
        result = (xblk[tick, pl.ds(n * GROUPS, GROUPS)].astype(F32) + total).astype(BF)
        xnew = pl.ds(n * GROUPS, GROUPS)
        for g in range(GROUPS):
            start = pl.multiple_of(n * PART + g * COL, COL)
            made[tick, :, pl.ds(start, COL)] = result[g]

        @pl.when(tick == 0)
        def _():
            perm_out[0, xnew] = result
            send(
                perm_out.at[0, xnew],
                perm_f.at[xnew],
                ps_sem.at[0],
                pr_sem.at[0],
                along_pipe(1),
            )

    def combine_backward(tick, n):
        dn[pl.ds(n * GROUPS, GROUPS)] = combine(2 * tick + 1, n)

    def hidden():
        gate_pre, up_pre = acc[0, 0], acc[0, 1]
        hid[0] = (gate_pre * jax.nn.sigmoid(gate_pre) * up_pre).astype(BF)

    def gradients():
        gate_pre, up_pre, grad_hidden = acc[1, 0], acc[1, 1], acc_c[...]
        sigma = jax.nn.sigmoid(gate_pre)
        hid[1] = (grad_hidden * up_pre * sigma * (1.0 + gate_pre * (1.0 - sigma))).astype(BF)
        hid[2] = (grad_hidden * gate_pre * sigma).astype(BF)

    def finish_backward(tick):
        inverse = inv_b[tick][:, :1]
        inner = jnp.zeros((tokens, COL), F32)
        for b in range(blocks):
            gain_row = gain[:, b * COL : (b + 1) * COL].astype(F32)
            inner += sblk[tick, b].astype(F32) * (gain_row * dn[b])
        inner = jnp.sum(inner, axis=1, keepdims=True) * (1.0 / width)
        factor = inverse * inverse * inverse * inner
        for b in range(blocks):
            gain_row = gain[:, b * COL : (b + 1) * COL].astype(F32)
            result = cblk[tick, b].astype(F32) + inverse * (gain_row * dn[b])
            result = (result - sblk[tick, b].astype(F32) * factor).astype(BF)
            grad[tick, :, b * COL : (b + 1) * COL] = result
            perm_out[1, b] = result

        @pl.when(tick == 0)
        def _():
            send(perm_out.at[1], perm_b, ps_sem.at[1], pr_sem.at[1], along_pipe(-1))

    def step(s, carry):
        slot = s // parts

        @pl.when(s == 3)
        def _():
            for tick in range(TICKS):
                to_blocks(saved_b[tick], sblk, tick)
                leg = (LEG_B0, LEG_B1)[tick]
                inverse = norm_blocks(sblk, tick, leg)
                inv_b[tick] = jnp.broadcast_to(inverse, (tokens, COL))
            rows = hold_g[...]
            to_blocks(rows, cblk, 0)
            nblk[LEG_C0] = cblk[0]

        @pl.when(s == 4)
        def _():
            for copy in weights:
                copy.wait()

        @pl.when((s == 11) | (s == 53))
        def _():
            hidden()

        @pl.when((s == 25) | (s == 60))
        def _():
            gradients()

        @pl.when(s == 42)
        def _():
            wait_for(perm_f, pr_sem.at[0])
            to_blocks(enter_a[...], xblk, 1)
            xblk[1] = jnp.where(pipe == 0, xblk[1], perm_f[...])
            norm_blocks(xblk, 1, LEG_F1)

        @pl.when((s == 44) | (s == 76))
        def _():
            finish_backward(s // 76)

        @pl.when(s == 49)
        def _():
            wait_for(perm_b, pr_sem.at[1])
            wait_for(perm_out.at[1], ps_sem.at[1])
            to_blocks(enter_g[...], cblk, 1)
            cblk[1] = jnp.where(pipe == n_pipe - 1, cblk[1], perm_b[...])
            nblk[LEG_C1] = cblk[1]

        @pl.when(between(s, 2, 23) | between(s, 37, 58))
        def _():
            turn = (s - 2) // parts
            spread(jnp.where(turn < 3, turn, turn - 2), (s - 2) % parts)

        @pl.when(between(s, 23, 30) | between(s, 58, 65))
        def _():
            out_forward((s // 58) * 2, (s - 23) % parts)

        @pl.when(between(s, 30, 37) | between(s, 65, 72))
        def _():
            out_backward((s // 65) * 2 + 1, (s - 23) % parts)

        @pl.when(between(s, 28, 42))
        def _():
            gather_back((s - 28) // parts, (s - 28) % parts)

        @pl.when(between(s, 60, 74))
        def _():
            gather_back((s - 60) // parts + 2, (s - 60) % parts)

        @pl.when(between(s, 0, 28) | between(s, 42, 56))
        def _():
            select(jnp.where(slot < 4, slot, slot - 2), s % parts)

        @pl.when(between(s, 30, 37) | between(s, 62, 69))
        def _():
            combine_forward(s // 62, (s - 30 - (s // 62) * 32) % parts)

        @pl.when(between(s, 37, 44) | between(s, 69, 76))
        def _():
            combine_backward(s // 69, (s - 37 - (s // 69) * 32) % parts)

        @pl.when(between(s, 4, 18) | between(s, 39, 53))
        def _():
            turn = (s - 4) // parts
            leg = jnp.where(turn < 2, turn, turn - 2)
            expert_in(leg, (s - 4) % parts, leg % 2)

        @pl.when(between(s, 18, 25) | between(s, 53, 60))
        def _():
            turn = (s - 4) // parts
            expert_cot(jnp.where(turn < 3, turn, turn - 2), (s - 4) % parts)

        return carry

    lax.fori_loop(0, 77, step, 0)

    for leg in range(LEGS):
        wait_for(zsend.at[leg, :, pl.ds(1, PEERS - 1)], zs_sem.at[leg])
        wait_for(xin.at[leg, :, pl.ds(1, XN - 1)], xs_sem.at[leg])
    for leg in range(RETURNS):
        wait_for(zback.at[leg, :, pl.ds(1, PEERS - 1)], zs_sem.at[LEGS + leg])
        wait_for(oute.at[leg, :, pl.ds(1, XN - 1)], xs_sem.at[LEGS + leg])
    wait_for(perm_out.at[0], ps_sem.at[0])


def body(
    hold_a,
    enter_a,
    saved_b,
    hold_g,
    enter_g,
    gain,
    w_gate,
    w_up,
    w_down,
    route_a,
    gate_a,
    route_b,
    gate_b,
):
    tokens, width = enter_a.shape
    hidden_units = w_down.shape[1]
    parts = width // PART
    blocks = parts * GROUPS
    route = jnp.concatenate([route_a[:, 0], route_b[:, 0]], axis=0)
    gate = jnp.concatenate([gate_a[:, 0], gate_b[:, 0]], axis=0)
    plain, gated, plain_t, gated_t = route_tables(route, gate)
    sel = jnp.stack([plain[0], plain[2], gated[2], plain[3], plain[1], gated[3]])
    comb = jnp.stack([gated_t[0], plain_t[2], gated_t[1], plain_t[3]])
    p1, p2 = perm_tables()
    vmem = pl.BlockSpec(memory_space=pltpu.VMEM)
    hbm = pl.BlockSpec(memory_space=pl.ANY)
    rows = XN * SLOTS
    out = jax.ShapeDtypeStruct((TICKS, tokens, width), BF)
    token_blocks = (blocks, tokens, COL)
    z_block = (parts, PEERS, SLOTS, COL)
    made, grad = pl.pallas_call(
        functools.partial(kernel, parts),
        out_shape=(out, out),
        in_specs=[vmem] * 10 + [hbm] * 3,
        out_specs=(vmem, vmem),
        scratch_shapes=[
            pltpu.VMEM((parts, PART, hidden_units), BF),
            pltpu.VMEM((parts, PART, hidden_units), BF),
            pltpu.VMEM((hidden_units, width), BF),
            pltpu.VMEM((TICKS,) + token_blocks, BF),
            pltpu.VMEM((TICKS,) + token_blocks, BF),
            pltpu.VMEM((TICKS,) + token_blocks, BF),
            pltpu.VMEM((LEGS,) + token_blocks, BF),
            pltpu.VMEM((TICKS, tokens, COL), F32),
            pltpu.VMEM(token_blocks, F32),
            pltpu.VMEM(token_blocks, BF),
            pltpu.VMEM((2,) + token_blocks, BF),
            pltpu.VMEM(token_blocks, BF),
            pltpu.VMEM((LEGS,) + z_block, BF),
            pltpu.VMEM((LEGS,) + z_block, BF),
            pltpu.VMEM((LEGS, parts, 2, SLOTS, PART), BF),
            pltpu.VMEM((LEGS, parts, XN, SLOTS, PART), BF),
            pltpu.VMEM((RETURNS, parts, XN, SLOTS, PART), BF),
            pltpu.VMEM((RETURNS, parts, XN, SLOTS, PART), BF),
            pltpu.VMEM((RETURNS,) + z_block, BF),
            pltpu.VMEM((RETURNS,) + z_block, BF),
            pltpu.VMEM((2, 2, rows, hidden_units), F32),
            pltpu.VMEM((rows, hidden_units), F32),
            pltpu.VMEM((3, rows, hidden_units), BF),
            pltpu.SemaphoreType.DMA((3,)),
            pltpu.SemaphoreType.DMA((LEGS + RETURNS,)),
            pltpu.SemaphoreType.DMA((LEGS + RETURNS, parts)),
            pltpu.SemaphoreType.DMA((LEGS + RETURNS,)),
            pltpu.SemaphoreType.DMA((LEGS + RETURNS, parts)),
            pltpu.SemaphoreType.DMA((2,)),
            pltpu.SemaphoreType.DMA((2,)),
        ],
        compiler_params=pltpu.CompilerParams(
            collective_id=0, has_side_effects=True, vmem_limit_bytes=62 * 2**20
        ),
        name="relay",
    )(
        hold_a[0],
        enter_a,
        saved_b[:, 0],
        hold_g[0],
        enter_g,
        gain,
        sel,
        comb,
        jnp.asarray(p1, BF),
        jnp.asarray(p2, BF),
        w_gate[0].reshape(parts, PART, hidden_units),
        w_up[0].reshape(parts, PART, hidden_units),
        w_down[0],
    )
    return (made[:, None], grad[:, None])


def solution(mesh):
    placed = (
        P("pipe", "expert", None),
        P("expert", None),
        P(None, "pipe", "expert", None),
        P("pipe", "expert", None),
        P("expert", None),
        P("pipe", None),
        P("pipe", None, "expert"),
        P("pipe", None, "expert"),
        P("pipe", "expert", None),
        P(None, "pipe", "expert", None),
        P(None, "pipe", "expert", None),
        P(None, "pipe", "expert", None),
        P(None, "pipe", "expert", None),
    )
    return jax.shard_map(
        body,
        mesh=mesh,
        in_specs=placed,
        out_specs=(P(None, "pipe", "expert", None), P(None, "pipe", "expert", None)),
        check_vma=False,
    )
```

```python
import functools

import jax
import jax.numpy as jnp
from jax import lax
from jax.experimental import pallas as pl
from jax.experimental.pallas import tpu as pltpu
from jax.sharding import PartitionSpec as P

SLICES = 2
TOP = 2
TICKS = 2
CAP = 6
MESH = pl.DeviceIdType.MESH
BF = jnp.bfloat16
F32 = jnp.float32

epsilon = 1e-06
gate_unit = 1.0 / 256.0

XN = 4
ZN = 4
PEERS = 8
GROUPS = 4
SLOTS = 48
COL = 128
PART = GROUPS * COL
LAG_Z = 3
LAG_X = 2
GROUP_STEP = 1024
VMEM_MIB = 51
SENDING = 3
RETURNING = 2


def place_of(index):
    return index // (ZN * 2), (index // 2) % ZN, index % 2


def fields(row):
    six = (row * 10923) >> 16
    return (row * 21846) >> 20, ((row * 5462) >> 16) & (GROUPS - 1), six & 1, row - six * CAP


LEG_F0, LEG_B0, LEG_C0, LEG_B1, LEG_F1, LEG_C1 = range(6)
LEGS = 6
RETURNS = 4


RET_F0, RET_B0, RET_F1, RET_B1 = range(RETURNS)


def schedule(parts):
    x_order = [
        (LEG_F0, False),
        (LEG_B0, False),
        (LEG_C0, False),
        (RET_F0, True),
        (RET_B0, True),
        (LEG_B1, False),
        (LEG_F1, False),
        (LEG_C1, False),
        (RET_F1, True),
        (RET_B1, True),
    ]
    spread, give = {}, {}
    for turn, (leg, back) in enumerate(x_order):
        (give if back else spread)[leg] = LAG_Z + turn * parts
    arrive = {leg: first + LAG_X for leg, first in spread.items()}
    z_order = [LEG_F0, LEG_B0, LEG_C0, LEG_B1, None, None, LEG_F1, LEG_C1]
    select = {leg: turn * parts for turn, leg in enumerate(z_order) if leg is not None}
    gather, free = {}, 4 * parts
    for leg in range(RETURNS):
        if leg == RET_F1:
            free = 8 * parts
        gather[leg] = max(free, give[leg] + LAG_X)
        free = gather[leg] + parts
    combine = {leg: first + LAG_Z for leg, first in gather.items()}
    plan = {
        "prepare": 4,
        "weights": arrive[LEG_F0],
        "hidden": (arrive[LEG_F0] + parts, arrive[LEG_F1] + parts),
        "gradients": (arrive[LEG_C0] + parts, arrive[LEG_C1] + parts),
        "enter_f": select[LEG_F1],
        "enter_b": select[LEG_C1],
        "finish": (combine[RET_B0] + parts, combine[RET_B1] + parts),
        "spread": [(spread[leg], leg) for leg in range(LEGS)],
        "out_forward": [(give[leg], leg) for leg in (RET_F0, RET_F1)],
        "out_backward": [(give[leg], leg) for leg in (RET_B0, RET_B1)],
        "gather_back": [(gather[leg], leg) for leg in range(RETURNS)],
        "select": [(select[leg], leg) for leg in range(LEGS)],
        "combine_forward": [(combine[leg], leg // 2) for leg in (RET_F0, RET_F1)],
        "combine_backward": [(combine[leg], leg // 2) for leg in (RET_B0, RET_B1)],
        "expert_in": [(arrive[leg], leg) for leg in (LEG_F0, LEG_B0, LEG_B1, LEG_F1)],
        "expert_cot": [(arrive[leg], leg) for leg in (LEG_C0, LEG_C1)],
    }
    return plan


def kernel(
    parts,
    hold_a_hbm,
    enter_a_hbm,
    saved_b_hbm,
    hold_g_hbm,
    enter_g_hbm,
    gain_hbm,
    route_a_hbm,
    gate_a_hbm,
    route_b_hbm,
    gate_b_hbm,
    wg_hbm,
    wu_hbm,
    wd_hbm,
    made,
    grad,
    hold_a,
    enter_a,
    saved_b,
    hold_g,
    enter_g,
    gain,
    route_a,
    gate_a,
    route_b,
    gate_b,
    wg,
    wu,
    wd,
    xblk,
    sblk,
    cblk,
    nblk,
    inv_b,
    dn,
    perm_f,
    perm_out,
    perm_b,
    zsend,
    zrecv,
    xout,
    xin,
    oute,
    xret,
    zback,
    zret,
    acc,
    acc_c,
    hid,
    sel,
    comb,
    p1,
    p2,
    w_sem,
    zs_sem,
    zr_sem,
    xs_sem,
    xr_sem,
    ps_sem,
    pr_sem,
):
    n_pipe = lax.axis_size("pipe")
    pipe = lax.axis_index("pipe")
    x, z, c = place_of(lax.axis_index("expert"))
    tokens = hold_a.shape[0]
    width = parts * PART
    blocks = parts * GROUPS

    def along_z(r, sign):
        return (pipe, x * (ZN * 2) + (z + ZN + sign * (r // 2)) % ZN * 2 + (c + r % 2) % 2)

    def along_x(dx, sign):
        return (pipe, (x + XN + sign * dx) % XN * (ZN * 2) + z * 2 + c)

    def along_pipe(sign):
        return ((pipe + n_pipe + sign) % n_pipe, lax.axis_index("expert"))

    pairs = [
        (hold_a_hbm, hold_a),
        (gain_hbm, gain),
        (route_a_hbm, route_a),
        (gate_a_hbm, gate_a),
        (route_b_hbm, route_b),
        (gate_b_hbm, gate_b),
        (saved_b_hbm, saved_b),
        (hold_g_hbm, hold_g),
        (wg_hbm, wg),
        (wu_hbm, wu),
        (wd_hbm, wd),
        (enter_a_hbm, enter_a),
        (enter_g_hbm, enter_g),
    ]
    loads = [pltpu.make_async_copy(*pair, w_sem.at[i]) for i, pair in enumerate(pairs)]
    for copy in loads:
        copy.start()

    barrier = pltpu.get_barrier_semaphore()
    greeted = [along_z(r, 1) for r in range(1, PEERS)]
    greeted += [along_x(dx, 1) for dx in range(1, XN)]
    greeted += [along_pipe(1), along_pipe(-1)]
    for peer in greeted:
        pl.semaphore_signal(barrier, inc=1, device_id=peer, device_id_type=MESH)

    def to_blocks(rows, ref, tick):
        for b in range(blocks):
            ref[tick, b] = rows[:, b * COL : (b + 1) * COL]

    def norm_blocks(ref, tick, leg):
        as_float = ref[tick].astype(F32)
        square = jnp.sum(jnp.sum(as_float * as_float, axis=0), axis=1, keepdims=True)
        inverse = lax.rsqrt(square * (1.0 / width) + epsilon)
        for b in range(blocks):
            gain_row = gain[:, b * COL : (b + 1) * COL].astype(F32)
            nblk[leg, b] = (as_float[b] * inverse * gain_row).astype(BF)
        return inverse

    def slot_of_row(row):
        r, group, q, slot = fields(row)
        expert = ((x + q) & 1) * (ZN * 2) + ((z + (r >> 1)) & (ZN - 1)) * 2 + ((c + r) & 1)
        return expert * CAP + slot + group * GROUP_STEP

    def make_p1():
        shape = (PEERS * SLOTS, PEERS * SLOTS)
        r, group, q, slot = fields(lax.broadcasted_iota(jnp.int32, (1, shape[1]), 1))
        target = (group * 2 + q) * SLOTS + r * CAP + slot
        hit = lax.broadcasted_iota(jnp.int32, shape, 0) == target
        p1[...] = jnp.where(hit, 1.0, 0.0).astype(BF)

    def make_p2():
        shape = (PEERS * SLOTS, GROUPS * XN * SLOTS)
        column = lax.broadcasted_iota(jnp.int32, (1, shape[1]), 1)
        block = (column * 21846) >> 20
        six = (column * 10923) >> 16
        target = (six & (PEERS - 1)) * SLOTS + (block >> 2) * 2 * CAP
        target += (block & 1) * CAP + column - six * CAP
        hit = lax.broadcasted_iota(jnp.int32, shape, 0) == target
        p2[...] = jnp.where(hit, 1.0, 0.0).astype(BF)

    def route_tables(route, gate, plain_to, gated_to, back_to, gate_back):
        row = [route[k : k + 1] for k in range(TOP)]
        token = lax.broadcasted_iota(jnp.int32, (tokens, tokens), 0)
        other = lax.broadcasted_iota(jnp.int32, (tokens, tokens), 1)
        col = [jnp.sum(jnp.where(token == other, v, 0), axis=1, keepdims=True) for v in row]
        slots = []
        for k in range(TOP):
            same = jnp.where((col[k] == row[k]) & (other < token), 1, 0)
            for j in range(k):
                same += jnp.where(col[k] == row[j], 1, 0)
            slots.append(col[k] * CAP + jnp.sum(same, axis=1, keepdims=True))
        shape = (GROUPS * tokens, GROUPS * tokens)
        down = lax.broadcasted_iota(jnp.int32, shape, 0)
        eye = down == lax.broadcasted_iota(jnp.int32, shape, 1)
        id_col, id_row, g_col, g_row = [], [], [], []
        for k in range(TOP):
            ids = [slots[k] + g * GROUP_STEP for g in range(GROUPS)]
            ids = jnp.concatenate(ids, axis=0)
            value = jnp.where(token == other, gate[k : k + 1], 0)
            value = jnp.sum(value, axis=1, keepdims=True).astype(F32) * gate_unit
            value = jnp.concatenate([value] * GROUPS, axis=0)
            id_col.append(ids)
            g_col.append(value)
            id_row.append(jnp.sum(jnp.where(eye, ids, 0), axis=0, keepdims=True))
            g_row.append(jnp.sum(jnp.where(eye, value, 0.0), axis=0, keepdims=True))
        own = slot_of_row(lax.broadcasted_iota(jnp.int32, (PEERS * SLOTS, 1), 0))
        hits = [own == v for v in id_row]
        if plain_to is not None:
            sel[plain_to] = jnp.where(hits[0] | hits[1], 1.0, 0.0).astype(BF)
        if gated_to is not None:
            gated = jnp.where(hits[0], g_row[0], jnp.where(hits[1], g_row[1], 0.0))
            sel[gated_to] = gated.astype(BF)
        own = slot_of_row(lax.broadcasted_iota(jnp.int32, (1, PEERS * SLOTS), 1))
        hits = [own == v for v in id_col]
        if gate_back:
            back = jnp.where(hits[0], g_col[0], jnp.where(hits[1], g_col[1], 0.0))
        else:
            back = jnp.where(hits[0] | hits[1], 1.0, 0.0)
        comb[back_to] = back.astype(BF)

    for copy in loads[:4]:
        copy.wait()
    to_blocks(hold_a[...], xblk, 0)
    norm_blocks(xblk, 0, LEG_F0)
    route_tables(route_a[0], gate_a[0], LEG_F0, None, RET_F0, True)
    pl.semaphore_wait(barrier, len(greeted))

    def send(src, dst, s_sem, r_sem, peer):
        pltpu.make_async_remote_copy(
            src_ref=src,
            dst_ref=dst,
            send_sem=s_sem,
            recv_sem=r_sem,
            device_id=peer,
            device_id_type=MESH,
        ).start()

    def wait_for(ref, sem):
        pltpu.make_async_copy(ref, ref, sem).wait()

    def between(s, low, high):
        return (s >= low) & (s < high)

    def select(leg, n):
        rows = nblk[leg, pl.ds(n * GROUPS, GROUPS)].reshape(GROUPS * tokens, COL)
        picked = jnp.dot(sel[leg], rows, preferred_element_type=F32).astype(BF)
        picked = picked.reshape(PEERS, SLOTS, COL)
        turn = lax.rem(leg, SENDING)

        @pl.when((leg >= SENDING) & (n == 0))
        def _():
            wait_for(zsend.at[turn, :, pl.ds(1, PEERS - 1)], zs_sem.at[leg - SENDING])

        zrecv[leg, n, 0] = picked[0]
        zsend[turn, n] = picked
        for r in (4, 5, 2, 3, 6, 7, 1):
            send(
                zsend.at[turn, n, r],
                zrecv.at[leg, n, r],
                zs_sem.at[leg],
                zr_sem.at[leg, n],
                along_z(r, 1),
            )

    def spread(leg, n):
        wait_for(zrecv.at[leg, n, pl.ds(1, PEERS - 1)], zr_sem.at[leg, n])
        rows = zrecv[leg, n].reshape(PEERS * SLOTS, COL)
        sorted_rows = jnp.dot(p1[...], rows, preferred_element_type=F32).astype(BF)
        sorted_rows = sorted_rows.reshape(GROUPS, 2, SLOTS, COL)
        turn = lax.rem(leg, SENDING)

        @pl.when((leg >= SENDING) & (n == 0))
        def _():
            wait_for(xin.at[leg, :, pl.ds(1, XN - 1)], xs_sem.at[leg - SENDING])

        for q in (1, 0):
            for g in range(GROUPS):
                xout[turn, n, q, :, g * COL : (g + 1) * COL] = sorted_rows[g, q]
                if q == 0:
                    xin[leg, n, 0, :, g * COL : (g + 1) * COL] = sorted_rows[g, q]
        for dx in (2, 1, 3):
            send(
                xout.at[turn, n, dx % 2],
                xin.at[leg, n, dx],
                xs_sem.at[leg],
                xr_sem.at[leg, n],
                along_x(dx, 1),
            )

    def wait_rows(leg, n):
        wait_for(xin.at[leg, n, pl.ds(1, XN - 1)], xr_sem.at[leg, n])
        return xin[leg, n].reshape(XN * SLOTS, PART)

    def expert_in(leg, n):
        rows = wait_rows(leg, n)
        back = lax.rem(leg, 2)
        for j, w in enumerate((wg, wu)):
            product = jnp.dot(rows, w[n], preferred_element_type=F32)
            acc[back, j] = jnp.where(n == 0, 0.0, acc[back, j]) + product

    def columns(n):
        return pl.ds(pl.multiple_of(n * PART, PART), PART)

    contract = (((1,), (1,)), ((), ()))

    def expert_cot(leg, n):
        rows = wait_rows(leg, n)
        product = lax.dot_general(rows, wd[:, columns(n)], contract, preferred_element_type=F32)
        acc_c[...] = jnp.where(n == 0, 0.0, acc_c[...]) + product

    def give_back(leg, n, piece):
        piece = piece.astype(BF).reshape(XN, SLOTS, PART)
        turn = lax.rem(leg, RETURNING)

        @pl.when((leg >= RETURNING) & (n == 0))
        def _():
            wait_for(oute.at[turn, :, pl.ds(1, XN - 1)], xs_sem.at[LEGS + leg - RETURNING])

        xret[leg, n, 0] = piece[0]
        oute[turn, n] = piece
        for dx in (2, 1, 3):
            send(
                oute.at[turn, n, dx],
                xret.at[leg, n, dx],
                xs_sem.at[LEGS + leg],
                xr_sem.at[LEGS + leg, n],
                along_x(dx, -1),
            )

    def out_forward(leg, n):
        give_back(leg, n, jnp.dot(hid[0], wd[:, columns(n)], preferred_element_type=F32))

    def out_backward(leg, n):
        piece = lax.dot_general(hid[1], wg[n], contract, preferred_element_type=F32)
        piece += lax.dot_general(hid[2], wu[n], contract, preferred_element_type=F32)
        give_back(leg, n, piece)

    def gather_back(leg, n):
        wait_for(xret.at[leg, n, pl.ds(1, XN - 1)], xr_sem.at[LEGS + leg, n])
        rows = xret[leg, n].reshape(XN * SLOTS, PART)
        stacked = jnp.concatenate(
            [rows[:, g * COL : (g + 1) * COL] for g in range(GROUPS)], axis=0
        )
        sums = jnp.dot(p2[...], stacked, preferred_element_type=F32).astype(BF)
        sums = sums.reshape(PEERS, SLOTS, COL)
        turn = lax.rem(leg, RETURNING)

        @pl.when((leg >= RETURNING) & (n == 0))
        def _():
            wait_for(zback.at[turn, :, pl.ds(1, PEERS - 1)], zs_sem.at[LEGS + leg - RETURNING])

        zret[leg, n, 0] = sums[0]
        zback[turn, n] = sums
        for r in (4, 5, 2, 3, 6, 7, 1):
            send(
                zback.at[turn, n, r],
                zret.at[leg, n, r],
                zs_sem.at[LEGS + leg],
                zr_sem.at[LEGS + leg, n],
                along_z(r, -1),
            )

    def combine(leg, n):
        wait_for(zret.at[leg, n, pl.ds(1, PEERS - 1)], zr_sem.at[LEGS + leg, n])
        rows = zret[leg, n].reshape(PEERS * SLOTS, COL)
        total = jnp.dot(comb[leg], rows, preferred_element_type=F32)
        return total.reshape(GROUPS, tokens, COL)

    def combine_forward(tick, n):
        total = combine(2 * tick, n)
        result = (xblk[tick, pl.ds(n * GROUPS, GROUPS)].astype(F32) + total).astype(BF)
        xnew = pl.ds(n * GROUPS, GROUPS)
        for g in range(GROUPS):
            start = pl.multiple_of(n * PART + g * COL, COL)
            made[tick, :, pl.ds(start, COL)] = result[g]

        @pl.when(tick == 0)
        def _():
            perm_out[0, xnew] = result
            send(
                perm_out.at[0, xnew],
                perm_f.at[xnew],
                ps_sem.at[0],
                pr_sem.at[0],
                along_pipe(1),
            )

    def combine_backward(tick, n):
        dn[pl.ds(n * GROUPS, GROUPS)] = combine(2 * tick + 1, n)

    def hidden():
        gate_pre, up_pre = acc[0, 0], acc[0, 1]
        hid[0] = (gate_pre * jax.nn.sigmoid(gate_pre) * up_pre).astype(BF)

    def gradients():
        gate_pre, up_pre, grad_hidden = acc[1, 0], acc[1, 1], acc_c[...]
        sigma = jax.nn.sigmoid(gate_pre)
        hid[1] = (grad_hidden * up_pre * sigma * (1.0 + gate_pre * (1.0 - sigma))).astype(BF)
        hid[2] = (grad_hidden * gate_pre * sigma).astype(BF)

    def finish_backward(tick):
        inverse = inv_b[tick][:, :1]
        inner = jnp.zeros((tokens, COL), F32)
        for b in range(blocks):
            gain_row = gain[:, b * COL : (b + 1) * COL].astype(F32)
            inner += sblk[tick, b].astype(F32) * (gain_row * dn[b])
        inner = jnp.sum(inner, axis=1, keepdims=True) * (1.0 / width)
        factor = inverse * inverse * inverse * inner
        for b in range(blocks):
            gain_row = gain[:, b * COL : (b + 1) * COL].astype(F32)
            result = cblk[tick, b].astype(F32) + inverse * (gain_row * dn[b])
            result = (result - sblk[tick, b].astype(F32) * factor).astype(BF)
            grad[tick, :, b * COL : (b + 1) * COL] = result
            perm_out[1, b] = result

        @pl.when(tick == 0)
        def _():
            send(perm_out.at[1], perm_b, ps_sem.at[1], pr_sem.at[1], along_pipe(-1))

    def run(s, runs, task):
        active, leg, start = False, 0, 0
        for first, number in runs:
            active = active | between(s, first, first + parts)
            leg = jnp.where(s >= first, number, leg)
            start = jnp.where(s >= first, first, start)

        @pl.when(active)
        def _():
            task(leg, lax.rem(s - start, parts))

    plan = schedule(parts)

    def step(s, carry):
        @pl.when(s == plan["spread"][0][0] - 1)
        def _():
            make_p1()

        @pl.when(s == plan["prepare"])
        def _():
            for copy in loads[4:8]:
                copy.wait()
            for tick in range(TICKS):
                to_blocks(saved_b[tick], sblk, tick)
                leg = (LEG_B0, LEG_B1)[tick]
                inverse = norm_blocks(sblk, tick, leg)
                inv_b[tick] = jnp.broadcast_to(inverse, (tokens, COL))
                legs = ((LEG_B0, LEG_C0, RET_B0), (LEG_B1, LEG_C1, RET_B1))[tick]
                route_tables(route_b[tick], gate_b[tick], *legs, False)
            to_blocks(hold_g[...], cblk, 0)
            nblk[LEG_C0] = cblk[0]
            route_tables(route_a[1], gate_a[1], LEG_F1, None, RET_F1, True)
            make_p2()

        @pl.when(s == plan["weights"])
        def _():
            for copy in loads[8:]:
                copy.wait()

        @pl.when((s == plan["hidden"][0]) | (s == plan["hidden"][1]))
        def _():
            hidden()

        @pl.when((s == plan["gradients"][0]) | (s == plan["gradients"][1]))
        def _():
            gradients()

        @pl.when(s == plan["enter_f"])
        def _():
            wait_for(perm_f, pr_sem.at[0])
            to_blocks(enter_a[...], xblk, 1)
            xblk[1] = jnp.where(pipe == 0, xblk[1], perm_f[...])
            norm_blocks(xblk, 1, LEG_F1)

        @pl.when((s == plan["finish"][0]) | (s == plan["finish"][1]))
        def _():
            finish_backward(s // plan["finish"][1])

        @pl.when(s == plan["enter_b"])
        def _():
            wait_for(perm_b, pr_sem.at[1])
            wait_for(perm_out.at[1], ps_sem.at[1])
            to_blocks(enter_g[...], cblk, 1)
            cblk[1] = jnp.where(pipe == n_pipe - 1, cblk[1], perm_b[...])
            nblk[LEG_C1] = cblk[1]

        run(s, plan["out_forward"], out_forward)
        run(s, plan["out_backward"], out_backward)
        run(s, plan["select"], select)
        run(s, plan["spread"], spread)
        run(s, plan["gather_back"], gather_back)
        run(s, plan["combine_forward"], combine_forward)
        run(s, plan["combine_backward"], combine_backward)
        run(s, plan["expert_in"], expert_in)
        run(s, plan["expert_cot"], expert_cot)
        return carry

    lax.fori_loop(0, plan["finish"][1] + 1, step, 0)

    for leg in range(LEGS - SENDING, LEGS):
        wait_for(zsend.at[leg % SENDING, :, pl.ds(1, PEERS - 1)], zs_sem.at[leg])
        wait_for(xin.at[leg, :, pl.ds(1, XN - 1)], xs_sem.at[leg])
    for leg in range(RETURNS - RETURNING, RETURNS):
        turn = leg % RETURNING
        wait_for(zback.at[turn, :, pl.ds(1, PEERS - 1)], zs_sem.at[LEGS + leg])
        wait_for(oute.at[turn, :, pl.ds(1, XN - 1)], xs_sem.at[LEGS + leg])
    wait_for(perm_out.at[0], ps_sem.at[0])


def body(
    hold_a,
    enter_a,
    saved_b,
    hold_g,
    enter_g,
    gain,
    w_gate,
    w_up,
    w_down,
    route_a,
    gate_a,
    route_b,
    gate_b,
):
    tokens, width = enter_a.shape
    hidden_units = w_down.shape[1]
    parts = width // PART
    blocks = parts * GROUPS
    route_a, gate_a, route_b, gate_b = (
        v[:, 0].transpose(0, 2, 1) for v in (route_a, gate_a, route_b, gate_b)
    )
    vmem = pl.BlockSpec(memory_space=pltpu.VMEM)
    hbm = pl.BlockSpec(memory_space=pltpu.HBM)
    rows = XN * SLOTS
    out = jax.ShapeDtypeStruct((TICKS, tokens, width), BF)
    token_blocks = (blocks, tokens, COL)
    z_block = (parts, PEERS, SLOTS, COL)
    operands = (
        hold_a[0],
        enter_a,
        saved_b[:, 0],
        hold_g[0],
        enter_g,
        gain,
        route_a,
        gate_a,
        route_b,
        gate_b,
        w_gate[0].reshape(parts, PART, hidden_units),
        w_up[0].reshape(parts, PART, hidden_units),
        w_down[0],
    )
    made, grad = pl.pallas_call(
        functools.partial(kernel, parts),
        out_shape=(out, out),
        in_specs=[hbm] * 13,
        out_specs=(vmem, vmem),
        scratch_shapes=[
            pltpu.VMEM((tokens, width), BF),
            pltpu.VMEM((tokens, width), BF),
            pltpu.VMEM((TICKS, tokens, width), BF),
            pltpu.VMEM((tokens, width), BF),
            pltpu.VMEM((tokens, width), BF),
            pltpu.VMEM((1, width), BF),
            pltpu.VMEM((TICKS, TOP, tokens), jnp.int32),
            pltpu.VMEM((TICKS, TOP, tokens), jnp.int32),
            pltpu.VMEM((TICKS, TOP, tokens), jnp.int32),
            pltpu.VMEM((TICKS, TOP, tokens), jnp.int32),
            pltpu.VMEM((parts, PART, hidden_units), BF),
            pltpu.VMEM((parts, PART, hidden_units), BF),
            pltpu.VMEM((hidden_units, width), BF),
            pltpu.VMEM((TICKS,) + token_blocks, BF),
            pltpu.VMEM((TICKS,) + token_blocks, BF),
            pltpu.VMEM((TICKS,) + token_blocks, BF),
            pltpu.VMEM((LEGS,) + token_blocks, BF),
            pltpu.VMEM((TICKS, tokens, COL), F32),
            pltpu.VMEM(token_blocks, F32),
            pltpu.VMEM(token_blocks, BF),
            pltpu.VMEM((2,) + token_blocks, BF),
            pltpu.VMEM(token_blocks, BF),
            pltpu.VMEM((SENDING,) + z_block, BF),
            pltpu.VMEM((LEGS,) + z_block, BF),
            pltpu.VMEM((SENDING, parts, 2, SLOTS, PART), BF),
            pltpu.VMEM((LEGS, parts, XN, SLOTS, PART), BF),
            pltpu.VMEM((RETURNING, parts, XN, SLOTS, PART), BF),
            pltpu.VMEM((RETURNS, parts, XN, SLOTS, PART), BF),
            pltpu.VMEM((RETURNING,) + z_block, BF),
            pltpu.VMEM((RETURNS,) + z_block, BF),
            pltpu.VMEM((2, 2, rows, hidden_units), F32),
            pltpu.VMEM((rows, hidden_units), F32),
            pltpu.VMEM((3, rows, hidden_units), BF),
            pltpu.VMEM((LEGS, PEERS * SLOTS, GROUPS * tokens), BF),
            pltpu.VMEM((RETURNS, GROUPS * tokens, PEERS * SLOTS), BF),
            pltpu.VMEM((PEERS * SLOTS, PEERS * SLOTS), BF),
            pltpu.VMEM((PEERS * SLOTS, GROUPS * XN * SLOTS), BF),
            pltpu.SemaphoreType.DMA((13,)),
            pltpu.SemaphoreType.DMA((LEGS + RETURNS,)),
            pltpu.SemaphoreType.DMA((LEGS + RETURNS, parts)),
            pltpu.SemaphoreType.DMA((LEGS + RETURNS,)),
            pltpu.SemaphoreType.DMA((LEGS + RETURNS, parts)),
            pltpu.SemaphoreType.DMA((2,)),
            pltpu.SemaphoreType.DMA((2,)),
        ],
        compiler_params=pltpu.CompilerParams(
            collective_id=0, has_side_effects=True, vmem_limit_bytes=VMEM_MIB * 2**20
        ),
        name="relay",
    )(*[pltpu.with_memory_space_constraint(v, pltpu.HBM) for v in operands])
    return (made[:, None], grad[:, None])


def solution(mesh):
    placed = (
        P("pipe", "expert", None),
        P("expert", None),
        P(None, "pipe", "expert", None),
        P("pipe", "expert", None),
        P("expert", None),
        P("pipe", None),
        P("pipe", None, "expert"),
        P("pipe", None, "expert"),
        P("pipe", "expert", None),
        P(None, "pipe", "expert", None),
        P(None, "pipe", "expert", None),
        P(None, "pipe", "expert", None),
        P(None, "pipe", "expert", None),
    )
    return jax.shard_map(
        body,
        mesh=mesh,
        in_specs=placed,
        out_specs=(P(None, "pipe", "expert", None), P(None, "pipe", "expert", None)),
        check_vma=False,
    )
```

```python
import functools

import jax
import jax.numpy as jnp
from jax import lax
from jax.experimental import pallas as pl
from jax.experimental.pallas import tpu as pltpu
from jax.sharding import PartitionSpec as P

SLICES = 2
TOP = 2
TICKS = 2
CAP = 6
MESH = pl.DeviceIdType.MESH
BF = jnp.bfloat16
F32 = jnp.float32

epsilon = 1e-06
gate_unit = 1.0 / 256.0

XN = 4
ZN = 4
PEERS = 8
GROUPS = 4
SLOTS = 48
COL = 128
PART = GROUPS * COL
LAG_Z = 3
LAG_X = 2
GROUP_STEP = 1024
VMEM_MIB = 51
SENDING = 3
RETURNING = 2


def place_of(index):
    return index // (ZN * 2), (index // 2) % ZN, index % 2


def fields(row):
    six = (row * 10923) >> 16
    return (row * 21846) >> 20, ((row * 5462) >> 16) & (GROUPS - 1), six & 1, row - six * CAP


LEG_F0, LEG_B0, LEG_C0, LEG_B1, LEG_F1, LEG_C1 = range(6)
LEGS = 6
RETURNS = 4


RET_F0, RET_B0, RET_F1, RET_B1 = range(RETURNS)


def schedule(parts):
    x_order = [
        (LEG_F0, False),
        (LEG_B0, False),
        (LEG_C0, False),
        (RET_F0, True),
        (RET_B0, True),
        (LEG_B1, False),
        (LEG_F1, False),
        (LEG_C1, False),
        (RET_F1, True),
        (RET_B1, True),
    ]
    spread, give = {}, {}
    for turn, (leg, back) in enumerate(x_order):
        (give if back else spread)[leg] = LAG_Z + turn * parts
    arrive = {leg: first + LAG_X for leg, first in spread.items()}
    z_order = [LEG_F0, LEG_B0, LEG_C0, LEG_B1, None, None, LEG_F1, LEG_C1]
    select = {leg: turn * parts for turn, leg in enumerate(z_order) if leg is not None}
    gather, free = {}, 4 * parts
    for leg in range(RETURNS):
        if leg == RET_F1:
            free = 8 * parts
        gather[leg] = max(free, give[leg] + LAG_X)
        free = gather[leg] + parts
    combine = {leg: first + LAG_Z for leg, first in gather.items()}
    plan = {
        "prepare": 4,
        "weights": arrive[LEG_F0],
        "hidden": (arrive[LEG_F0] + parts, arrive[LEG_F1] + parts),
        "gradients": (arrive[LEG_C0] + parts, arrive[LEG_C1] + parts),
        "enter_f": select[LEG_F1],
        "enter_b": select[LEG_C1],
        "finish": (combine[RET_B0] + parts, combine[RET_B1] + parts),
        "spread": [(spread[leg], leg) for leg in range(LEGS)],
        "out_forward": [(give[leg], leg) for leg in (RET_F0, RET_F1)],
        "out_backward": [(give[leg], leg) for leg in (RET_B0, RET_B1)],
        "gather_back": [(gather[leg], leg) for leg in range(RETURNS)],
        "select": [(select[leg], leg) for leg in range(LEGS)],
        "combine_forward": [(combine[leg], leg // 2) for leg in (RET_F0, RET_F1)],
        "combine_backward": [(combine[leg], leg // 2) for leg in (RET_B0, RET_B1)],
        "expert_in": [(arrive[leg], leg) for leg in (LEG_F0, LEG_B0, LEG_B1, LEG_F1)],
        "expert_cot": [(arrive[leg], leg) for leg in (LEG_C0, LEG_C1)],
    }
    return plan


def kernel(
    parts,
    hold_a_hbm,
    enter_a_hbm,
    saved_b_hbm,
    hold_g_hbm,
    enter_g_hbm,
    gain_hbm,
    route_a_hbm,
    gate_a_hbm,
    route_b_hbm,
    gate_b_hbm,
    wg_hbm,
    wu_hbm,
    wd_hbm,
    results,
    hold_a,
    enter_a,
    saved_b,
    hold_g,
    enter_g,
    gain,
    route_a,
    gate_a,
    route_b,
    gate_b,
    wg,
    wu,
    wd,
    xblk,
    sblk,
    cblk,
    nblk,
    inv_b,
    dn,
    perm_f,
    perm_out,
    perm_b,
    zsend,
    zrecv,
    xout,
    xin,
    oute,
    xret,
    zback,
    zret,
    acc,
    acc_c,
    hid,
    sel,
    comb,
    p1,
    p2,
    w_sem,
    zs_sem,
    zr_sem,
    xs_sem,
    xr_sem,
    ps_sem,
    pr_sem,
):
    n_pipe = lax.axis_size("pipe")
    pipe = lax.axis_index("pipe")
    x, z, c = place_of(lax.axis_index("expert"))
    tokens = hold_a.shape[0]
    width = parts * PART
    blocks = parts * GROUPS

    def along_z(r, sign):
        return (pipe, x * (ZN * 2) + (z + ZN + sign * (r // 2)) % ZN * 2 + (c + r % 2) % 2)

    def along_x(dx, sign):
        return (pipe, (x + XN + sign * dx) % XN * (ZN * 2) + z * 2 + c)

    def along_pipe(sign):
        return ((pipe + n_pipe + sign) % n_pipe, lax.axis_index("expert"))

    pairs = [
        (hold_a_hbm, hold_a),
        (gain_hbm, gain),
        (route_a_hbm, route_a),
        (gate_a_hbm, gate_a),
        (route_b_hbm, route_b),
        (gate_b_hbm, gate_b),
        (saved_b_hbm, saved_b),
        (hold_g_hbm, hold_g),
        (wg_hbm, wg),
        (wu_hbm, wu),
        (wd_hbm, wd),
        (enter_a_hbm, enter_a),
        (enter_g_hbm, enter_g),
    ]
    loads = [pltpu.make_async_copy(*pair, w_sem.at[i]) for i, pair in enumerate(pairs)]
    for copy in loads:
        copy.start()

    barrier = pltpu.get_barrier_semaphore()
    greeted = [along_z(r, 1) for r in range(1, PEERS)]
    greeted += [along_x(dx, 1) for dx in range(1, XN)]
    greeted += [along_pipe(1), along_pipe(-1)]
    for peer in greeted:
        pl.semaphore_signal(barrier, inc=1, device_id=peer, device_id_type=MESH)

    def to_blocks(rows, ref, tick):
        for b in range(blocks):
            ref[tick, b] = rows[:, b * COL : (b + 1) * COL]

    def norm_blocks(ref, tick, leg):
        as_float = ref[tick].astype(F32)
        square = jnp.sum(jnp.sum(as_float * as_float, axis=0), axis=1, keepdims=True)
        inverse = lax.rsqrt(square * (1.0 / width) + epsilon)
        for b in range(blocks):
            gain_row = gain[:, b * COL : (b + 1) * COL].astype(F32)
            nblk[leg, b] = (as_float[b] * inverse * gain_row).astype(BF)
        return inverse

    def slot_of_row(row):
        r, group, q, slot = fields(row)
        expert = ((x + q) & 1) * (ZN * 2) + ((z + (r >> 1)) & (ZN - 1)) * 2 + ((c + r) & 1)
        return expert * CAP + slot + group * GROUP_STEP

    def make_p1():
        shape = (PEERS * SLOTS, PEERS * SLOTS)
        r, group, q, slot = fields(lax.broadcasted_iota(jnp.int32, (1, shape[1]), 1))
        target = (group * 2 + q) * SLOTS + r * CAP + slot
        hit = lax.broadcasted_iota(jnp.int32, shape, 0) == target
        p1[...] = jnp.where(hit, 1.0, 0.0).astype(BF)

    def make_p2():
        shape = (PEERS * SLOTS, GROUPS * XN * SLOTS)
        column = lax.broadcasted_iota(jnp.int32, (1, shape[1]), 1)
        block = (column * 21846) >> 20
        six = (column * 10923) >> 16
        target = (six & (PEERS - 1)) * SLOTS + (block >> 2) * 2 * CAP
        target += (block & 1) * CAP + column - six * CAP
        hit = lax.broadcasted_iota(jnp.int32, shape, 0) == target
        p2[...] = jnp.where(hit, 1.0, 0.0).astype(BF)

    def route_tables(route, gate, plain_to, gated_to, back_to, gate_back):
        row = [route[k : k + 1] for k in range(TOP)]
        token = lax.broadcasted_iota(jnp.int32, (tokens, tokens), 0)
        other = lax.broadcasted_iota(jnp.int32, (tokens, tokens), 1)
        col = [jnp.sum(jnp.where(token == other, v, 0), axis=1, keepdims=True) for v in row]
        slots = []
        for k in range(TOP):
            same = jnp.where((col[k] == row[k]) & (other < token), 1, 0)
            for j in range(k):
                same += jnp.where(col[k] == row[j], 1, 0)
            slots.append(col[k] * CAP + jnp.sum(same, axis=1, keepdims=True))
        shape = (GROUPS * tokens, GROUPS * tokens)
        down = lax.broadcasted_iota(jnp.int32, shape, 0)
        eye = down == lax.broadcasted_iota(jnp.int32, shape, 1)
        id_col, id_row, g_col, g_row = [], [], [], []
        for k in range(TOP):
            ids = [slots[k] + g * GROUP_STEP for g in range(GROUPS)]
            ids = jnp.concatenate(ids, axis=0)
            value = jnp.where(token == other, gate[k : k + 1], 0)
            value = jnp.sum(value, axis=1, keepdims=True).astype(F32) * gate_unit
            value = jnp.concatenate([value] * GROUPS, axis=0)
            id_col.append(ids)
            g_col.append(value)
            id_row.append(jnp.sum(jnp.where(eye, ids, 0), axis=0, keepdims=True))
            g_row.append(jnp.sum(jnp.where(eye, value, 0.0), axis=0, keepdims=True))
        own = slot_of_row(lax.broadcasted_iota(jnp.int32, (PEERS * SLOTS, 1), 0))
        hits = [own == v for v in id_row]
        if plain_to is not None:
            sel[plain_to] = jnp.where(hits[0] | hits[1], 1.0, 0.0).astype(BF)
        if gated_to is not None:
            gated = jnp.where(hits[0], g_row[0], jnp.where(hits[1], g_row[1], 0.0))
            sel[gated_to] = gated.astype(BF)
        own = slot_of_row(lax.broadcasted_iota(jnp.int32, (1, PEERS * SLOTS), 1))
        hits = [own == v for v in id_col]
        if gate_back:
            back = jnp.where(hits[0], g_col[0], jnp.where(hits[1], g_col[1], 0.0))
        else:
            back = jnp.where(hits[0] | hits[1], 1.0, 0.0)
        comb[back_to] = back.astype(BF)

    for copy in loads[:4]:
        copy.wait()
    to_blocks(hold_a[...], xblk, 0)
    norm_blocks(xblk, 0, LEG_F0)
    route_tables(route_a[0], gate_a[0], LEG_F0, None, RET_F0, True)
    pl.semaphore_wait(barrier, len(greeted))

    def send(src, dst, s_sem, r_sem, peer):
        pltpu.make_async_remote_copy(
            src_ref=src,
            dst_ref=dst,
            send_sem=s_sem,
            recv_sem=r_sem,
            device_id=peer,
            device_id_type=MESH,
        ).start()

    def wait_for(ref, sem):
        pltpu.make_async_copy(ref, ref, sem).wait()

    def between(s, low, high):
        return (s >= low) & (s < high)

    def select(leg, n):
        rows = nblk[leg, pl.ds(n * GROUPS, GROUPS)].reshape(GROUPS * tokens, COL)
        picked = jnp.dot(sel[leg], rows, preferred_element_type=F32).astype(BF)
        picked = picked.reshape(PEERS, SLOTS, COL)
        turn = lax.rem(leg, SENDING)

        @pl.when((leg >= SENDING) & (n == 0))
        def _():
            wait_for(zsend.at[turn, :, pl.ds(1, PEERS - 1)], zs_sem.at[leg - SENDING])

        zrecv[leg, n, 0] = picked[0]
        zsend[turn, n] = picked
        for r in (4, 5, 2, 3, 6, 7, 1):
            send(
                zsend.at[turn, n, r],
                zrecv.at[leg, n, r],
                zs_sem.at[leg],
                zr_sem.at[leg, n],
                along_z(r, 1),
            )

    def spread(leg, n):
        wait_for(zrecv.at[leg, n, pl.ds(1, PEERS - 1)], zr_sem.at[leg, n])
        rows = zrecv[leg, n].reshape(PEERS * SLOTS, COL)
        sorted_rows = jnp.dot(p1[...], rows, preferred_element_type=F32).astype(BF)
        sorted_rows = sorted_rows.reshape(GROUPS, 2, SLOTS, COL)
        turn = lax.rem(leg, SENDING)

        @pl.when((leg >= SENDING) & (n == 0))
        def _():
            wait_for(xin.at[leg, :, pl.ds(1, XN - 1)], xs_sem.at[leg - SENDING])

        for q in (1, 0):
            for g in range(GROUPS):
                xout[turn, n, q, :, g * COL : (g + 1) * COL] = sorted_rows[g, q]
                if q == 0:
                    xin[leg, n, 0, :, g * COL : (g + 1) * COL] = sorted_rows[g, q]
        for dx in (1, 3, 2):
            send(
                xout.at[turn, n, dx % 2],
                xin.at[leg, n, dx],
                xs_sem.at[leg],
                xr_sem.at[leg, n],
                along_x(dx, 1),
            )

    def wait_rows(leg, n):
        wait_for(xin.at[leg, n, pl.ds(1, XN - 1)], xr_sem.at[leg, n])
        return xin[leg, n].reshape(XN * SLOTS, PART)

    def expert_in(leg, n):
        rows = wait_rows(leg, n)
        back = lax.rem(leg, 2)
        for j, w in enumerate((wg, wu)):
            product = jnp.dot(rows, w[n], preferred_element_type=F32)
            acc[back, j] = jnp.where(n == 0, 0.0, acc[back, j]) + product

    def columns(n):
        return pl.ds(pl.multiple_of(n * PART, PART), PART)

    contract = (((1,), (1,)), ((), ()))

    def expert_cot(leg, n):
        rows = wait_rows(leg, n)
        product = lax.dot_general(rows, wd[:, columns(n)], contract, preferred_element_type=F32)
        acc_c[...] = jnp.where(n == 0, 0.0, acc_c[...]) + product

    def give_back(leg, n, piece):
        piece = piece.astype(BF).reshape(XN, SLOTS, PART)
        turn = lax.rem(leg, RETURNING)

        @pl.when((leg >= RETURNING) & (n == 0))
        def _():
            wait_for(oute.at[turn, :, pl.ds(1, XN - 1)], xs_sem.at[LEGS + leg - RETURNING])

        xret[leg, n, 0] = piece[0]
        oute[turn, n] = piece
        for dx in (1, 3, 2):
            send(
                oute.at[turn, n, dx],
                xret.at[leg, n, dx],
                xs_sem.at[LEGS + leg],
                xr_sem.at[LEGS + leg, n],
                along_x(dx, -1),
            )

    def out_forward(leg, n):
        give_back(leg, n, jnp.dot(hid[0], wd[:, columns(n)], preferred_element_type=F32))

    def out_backward(leg, n):
        piece = lax.dot_general(hid[1], wg[n], contract, preferred_element_type=F32)
        piece += lax.dot_general(hid[2], wu[n], contract, preferred_element_type=F32)
        give_back(leg, n, piece)

    def gather_back(leg, n):
        wait_for(xret.at[leg, n, pl.ds(1, XN - 1)], xr_sem.at[LEGS + leg, n])
        rows = xret[leg, n].reshape(XN * SLOTS, PART)
        stacked = jnp.concatenate(
            [rows[:, g * COL : (g + 1) * COL] for g in range(GROUPS)], axis=0
        )
        sums = jnp.dot(p2[...], stacked, preferred_element_type=F32).astype(BF)
        sums = sums.reshape(PEERS, SLOTS, COL)
        turn = lax.rem(leg, RETURNING)

        @pl.when((leg >= RETURNING) & (n == 0))
        def _():
            wait_for(zback.at[turn, :, pl.ds(1, PEERS - 1)], zs_sem.at[LEGS + leg - RETURNING])

        zret[leg, n, 0] = sums[0]
        zback[turn, n] = sums
        for r in (4, 5, 2, 3, 6, 7, 1):
            send(
                zback.at[turn, n, r],
                zret.at[leg, n, r],
                zs_sem.at[LEGS + leg],
                zr_sem.at[LEGS + leg, n],
                along_z(r, -1),
            )

    def combine(leg, n):
        wait_for(zret.at[leg, n, pl.ds(1, PEERS - 1)], zr_sem.at[LEGS + leg, n])
        rows = zret[leg, n].reshape(PEERS * SLOTS, COL)
        total = jnp.dot(comb[leg], rows, preferred_element_type=F32)
        return total.reshape(GROUPS, tokens, COL)

    def combine_forward(tick, n):
        total = combine(2 * tick, n)
        result = (xblk[tick, pl.ds(n * GROUPS, GROUPS)].astype(F32) + total).astype(BF)
        xnew = pl.ds(n * GROUPS, GROUPS)
        for g in range(GROUPS):
            start = pl.multiple_of(n * PART + g * COL, COL)
            results[0, tick, :, pl.ds(start, COL)] = result[g]

        @pl.when(tick == 0)
        def _():
            perm_out[0, xnew] = result
            send(
                perm_out.at[0, xnew],
                perm_f.at[xnew],
                ps_sem.at[0],
                pr_sem.at[0],
                along_pipe(1),
            )

    def combine_backward(tick, n):
        dn[pl.ds(n * GROUPS, GROUPS)] = combine(2 * tick + 1, n)

    def hidden():
        gate_pre, up_pre = acc[0, 0], acc[0, 1]
        hid[0] = (gate_pre * jax.nn.sigmoid(gate_pre) * up_pre).astype(BF)

    def gradients():
        gate_pre, up_pre, grad_hidden = acc[1, 0], acc[1, 1], acc_c[...]
        sigma = jax.nn.sigmoid(gate_pre)
        hid[1] = (grad_hidden * up_pre * sigma * (1.0 + gate_pre * (1.0 - sigma))).astype(BF)
        hid[2] = (grad_hidden * gate_pre * sigma).astype(BF)

    def finish_backward(tick):
        inverse = inv_b[tick][:, :1]
        inner = jnp.zeros((tokens, COL), F32)
        for b in range(blocks):
            gain_row = gain[:, b * COL : (b + 1) * COL].astype(F32)
            inner += sblk[tick, b].astype(F32) * (gain_row * dn[b])
        inner = jnp.sum(inner, axis=1, keepdims=True) * (1.0 / width)
        factor = inverse * inverse * inverse * inner
        for b in range(blocks):
            gain_row = gain[:, b * COL : (b + 1) * COL].astype(F32)
            result = cblk[tick, b].astype(F32) + inverse * (gain_row * dn[b])
            result = (result - sblk[tick, b].astype(F32) * factor).astype(BF)
            results[1, tick, :, b * COL : (b + 1) * COL] = result
            perm_out[1, b] = result

        @pl.when(tick == 0)
        def _():
            send(perm_out.at[1], perm_b, ps_sem.at[1], pr_sem.at[1], along_pipe(-1))

    def run(s, runs, task):
        active, leg, start = False, 0, 0
        for first, number in runs:
            active = active | between(s, first, first + parts)
            leg = jnp.where(s >= first, number, leg)
            start = jnp.where(s >= first, first, start)

        @pl.when(active)
        def _():
            task(leg, lax.rem(s - start, parts))

    plan = schedule(parts)

    def step(s, carry):
        @pl.when(s == plan["spread"][0][0] - 1)
        def _():
            make_p1()

        @pl.when(s == plan["prepare"])
        def _():
            for copy in loads[4:8]:
                copy.wait()
            for tick in range(TICKS):
                to_blocks(saved_b[tick], sblk, tick)
                leg = (LEG_B0, LEG_B1)[tick]
                inverse = norm_blocks(sblk, tick, leg)
                inv_b[tick] = jnp.broadcast_to(inverse, (tokens, COL))
                legs = ((LEG_B0, LEG_C0, RET_B0), (LEG_B1, LEG_C1, RET_B1))[tick]
                route_tables(route_b[tick], gate_b[tick], *legs, False)
            to_blocks(hold_g[...], cblk, 0)
            nblk[LEG_C0] = cblk[0]
            route_tables(route_a[1], gate_a[1], LEG_F1, None, RET_F1, True)
            make_p2()

        @pl.when(s == plan["weights"])
        def _():
            for copy in loads[8:]:
                copy.wait()

        @pl.when((s == plan["hidden"][0]) | (s == plan["hidden"][1]))
        def _():
            hidden()

        @pl.when((s == plan["gradients"][0]) | (s == plan["gradients"][1]))
        def _():
            gradients()

        @pl.when(s == plan["enter_f"])
        def _():
            wait_for(perm_f, pr_sem.at[0])
            to_blocks(enter_a[...], xblk, 1)
            xblk[1] = jnp.where(pipe == 0, xblk[1], perm_f[...])
            norm_blocks(xblk, 1, LEG_F1)

        @pl.when((s == plan["finish"][0]) | (s == plan["finish"][1]))
        def _():
            finish_backward(s // plan["finish"][1])

        @pl.when(s == plan["enter_b"])
        def _():
            wait_for(perm_b, pr_sem.at[1])
            wait_for(perm_out.at[1], ps_sem.at[1])
            to_blocks(enter_g[...], cblk, 1)
            cblk[1] = jnp.where(pipe == n_pipe - 1, cblk[1], perm_b[...])
            nblk[LEG_C1] = cblk[1]

        run(s, plan["out_forward"], out_forward)
        run(s, plan["out_backward"], out_backward)
        run(s, plan["select"], select)
        run(s, plan["spread"], spread)
        run(s, plan["gather_back"], gather_back)
        run(s, plan["combine_forward"], combine_forward)
        run(s, plan["combine_backward"], combine_backward)
        run(s, plan["expert_in"], expert_in)
        run(s, plan["expert_cot"], expert_cot)
        return carry

    lax.fori_loop(0, plan["finish"][1] + 1, step, 0)

    for leg in range(LEGS - SENDING, LEGS):
        wait_for(zsend.at[leg % SENDING, :, pl.ds(1, PEERS - 1)], zs_sem.at[leg])
        wait_for(xin.at[leg, :, pl.ds(1, XN - 1)], xs_sem.at[leg])
    for leg in range(RETURNS - RETURNING, RETURNS):
        turn = leg % RETURNING
        wait_for(zback.at[turn, :, pl.ds(1, PEERS - 1)], zs_sem.at[LEGS + leg])
        wait_for(oute.at[turn, :, pl.ds(1, XN - 1)], xs_sem.at[LEGS + leg])
    wait_for(perm_out.at[0], ps_sem.at[0])


def body(
    hold_a,
    enter_a,
    saved_b,
    hold_g,
    enter_g,
    gain,
    w_gate,
    w_up,
    w_down,
    route_a,
    gate_a,
    route_b,
    gate_b,
):
    tokens, width = enter_a.shape
    hidden_units = w_down.shape[1]
    parts = width // PART
    blocks = parts * GROUPS
    route_a, gate_a, route_b, gate_b = (
        v[:, 0].transpose(0, 2, 1) for v in (route_a, gate_a, route_b, gate_b)
    )
    vmem = pl.BlockSpec(memory_space=pltpu.VMEM)
    hbm = pl.BlockSpec(memory_space=pltpu.HBM)
    rows = XN * SLOTS
    out = jax.ShapeDtypeStruct((2, TICKS, tokens, width), BF)
    token_blocks = (blocks, tokens, COL)
    z_block = (parts, PEERS, SLOTS, COL)
    operands = (
        hold_a[0],
        enter_a,
        saved_b[:, 0],
        hold_g[0],
        enter_g,
        gain,
        route_a,
        gate_a,
        route_b,
        gate_b,
        w_gate[0].reshape(parts, PART, hidden_units),
        w_up[0].reshape(parts, PART, hidden_units),
        w_down[0],
    )
    results = pl.pallas_call(
        functools.partial(kernel, parts),
        out_shape=out,
        in_specs=[hbm] * 13,
        out_specs=vmem,
        scratch_shapes=[
            pltpu.VMEM((tokens, width), BF),
            pltpu.VMEM((tokens, width), BF),
            pltpu.VMEM((TICKS, tokens, width), BF),
            pltpu.VMEM((tokens, width), BF),
            pltpu.VMEM((tokens, width), BF),
            pltpu.VMEM((1, width), BF),
            pltpu.VMEM((TICKS, TOP, tokens), jnp.int32),
            pltpu.VMEM((TICKS, TOP, tokens), jnp.int32),
            pltpu.VMEM((TICKS, TOP, tokens), jnp.int32),
            pltpu.VMEM((TICKS, TOP, tokens), jnp.int32),
            pltpu.VMEM((parts, PART, hidden_units), BF),
            pltpu.VMEM((parts, PART, hidden_units), BF),
            pltpu.VMEM((hidden_units, width), BF),
            pltpu.VMEM((TICKS,) + token_blocks, BF),
            pltpu.VMEM((TICKS,) + token_blocks, BF),
            pltpu.VMEM((TICKS,) + token_blocks, BF),
            pltpu.VMEM((LEGS,) + token_blocks, BF),
            pltpu.VMEM((TICKS, tokens, COL), F32),
            pltpu.VMEM(token_blocks, F32),
            pltpu.VMEM(token_blocks, BF),
            pltpu.VMEM((2,) + token_blocks, BF),
            pltpu.VMEM(token_blocks, BF),
            pltpu.VMEM((SENDING,) + z_block, BF),
            pltpu.VMEM((LEGS,) + z_block, BF),
            pltpu.VMEM((SENDING, parts, 2, SLOTS, PART), BF),
            pltpu.VMEM((LEGS, parts, XN, SLOTS, PART), BF),
            pltpu.VMEM((RETURNING, parts, XN, SLOTS, PART), BF),
            pltpu.VMEM((RETURNS, parts, XN, SLOTS, PART), BF),
            pltpu.VMEM((RETURNING,) + z_block, BF),
            pltpu.VMEM((RETURNS,) + z_block, BF),
            pltpu.VMEM((2, 2, rows, hidden_units), F32),
            pltpu.VMEM((rows, hidden_units), F32),
            pltpu.VMEM((3, rows, hidden_units), BF),
            pltpu.VMEM((LEGS, PEERS * SLOTS, GROUPS * tokens), BF),
            pltpu.VMEM((RETURNS, GROUPS * tokens, PEERS * SLOTS), BF),
            pltpu.VMEM((PEERS * SLOTS, PEERS * SLOTS), BF),
            pltpu.VMEM((PEERS * SLOTS, GROUPS * XN * SLOTS), BF),
            pltpu.SemaphoreType.DMA((13,)),
            pltpu.SemaphoreType.DMA((LEGS + RETURNS,)),
            pltpu.SemaphoreType.DMA((LEGS + RETURNS, parts)),
            pltpu.SemaphoreType.DMA((LEGS + RETURNS,)),
            pltpu.SemaphoreType.DMA((LEGS + RETURNS, parts)),
            pltpu.SemaphoreType.DMA((2,)),
            pltpu.SemaphoreType.DMA((2,)),
        ],
        compiler_params=pltpu.CompilerParams(
            collective_id=0, has_side_effects=True, vmem_limit_bytes=VMEM_MIB * 2**20
        ),
        name="relay",
    )(*[pltpu.with_memory_space_constraint(v, pltpu.HBM) for v in operands])
    return (results[0][:, None], results[1][:, None])


def solution(mesh):
    placed = (
        P("pipe", "expert", None),
        P("expert", None),
        P(None, "pipe", "expert", None),
        P("pipe", "expert", None),
        P("expert", None),
        P("pipe", None),
        P("pipe", None, "expert"),
        P("pipe", None, "expert"),
        P("pipe", "expert", None),
        P(None, "pipe", "expert", None),
        P(None, "pipe", "expert", None),
        P(None, "pipe", "expert", None),
        P(None, "pipe", "expert", None),
    )
    return jax.shard_map(
        body,
        mesh=mesh,
        in_specs=placed,
        out_specs=(P(None, "pipe", "expert", None), P(None, "pipe", "expert", None)),
        check_vma=False,
    )
```
